32 devices in a mesh: img: 4 (over y, x), band: 8 (over z, core).
Axes of the slice: x: 2, y: 2, z: 4, core: 2. Of those that a mesh axis runs over, the one named last changes fastest.
Arguments:
- latents: bfloat16 [4, 16, 64, 1120], P('img', 'band'), may hold values from -6 to 6
- tangents: bfloat16 [4, 16, 64, 1120], P('img', 'band'), may hold values from -6 to 6
- w_expand: bfloat16 [1120, 5632], P('img', 'band'), may hold values from -0.1875 to 0.1875
- b_expand: bfloat16 [5632], P('band'), may hold values from -3 to 3
- w_depth: bfloat16 [9, 5632], P(None, 'band'), may hold values from -2 to 2
- b_depth: bfloat16 [5632], P('band'), may hold values from -3 to 3
Outputs:
- gated: bfloat16 [4, 16, 64, 2816], P('img', 'band')
- gated_tangent: bfloat16 [4, 16, 64, 2816], P('img', 'band')
The draws below stay inside these ranges and needn't reach their ends.
All inputs are finite; a program needn't handle non-finite values.
Results may differ from the reference program's by a relative error of at most 0.0057.
Values may be sent and summed in bfloat16 or wider, within the bound.
A program may use at most 64 MiB of HBM per device.

```python
import jax
import jax.numpy as jnp
from jax import lax

C = 1120
H = 2816
COLS = 64
IMAGES = 4
ROWS = 16


def block_levels(stream_key, extent, shards, smallest, largest):
    factor_of = 1.0
    for dim, blocks in shards:
        draws = jax.random.uniform(jax.random.fold_in(jax.random.fold_in(stream_key, 6), dim), (blocks,), jnp.float32, smallest / len(shards), largest / len(shards))
        factor_of = factor_of * jnp.repeat(jnp.exp(draws), extent[dim] // blocks).reshape((-1,) + (1,) * (len(extent) - 1 - dim))
    return factor_of


def normal_values(stream_key, dims, spread, limit, pieces=(), dtype=jnp.bfloat16):
    drawn = spread * jax.random.normal(stream_key, dims, jnp.float32)
    if pieces:
        drawn = drawn * block_levels(stream_key, dims, pieces, -0.22, 0.18)
    return jnp.clip(drawn, -limit, limit).astype(dtype)


def setup_inputs(seed: int = 0) -> dict:
    keys = jax.random.split(jax.random.key(seed), 7)
    return {
        "latents": normal_values(keys[0], (IMAGES, ROWS, COLS, C), 1.0, 6.0, ((0, 4), (1, 8))),
        "tangents": normal_values(keys[1], (IMAGES, ROWS, COLS, C), 1.0, 6.0, ((0, 4), (1, 8))),
        "w_expand": normal_values(keys[2], (C, 2 * H), C ** -0.5, 0.1875, ((0, 4), (1, 8))),
        "b_expand": normal_values(keys[3], (2 * H,), 0.5, 3.0, ((0, 8),)),
        "w_depth": normal_values(keys[4], (9, 2 * H), 9 ** -0.5, 2.0, ((1, 8),)),
        "b_depth": normal_values(keys[5], (2 * H,), 0.5, 3.0, ((0, 8),)),
    }


def tangent_act(primal_pre, tangent_pre):
    sigmoid_v = jax.nn.sigmoid(primal_pre)
    value = primal_pre * sigmoid_v
    slope = sigmoid_v * (1.0 + primal_pre * (1.0 - sigmoid_v))
    return value, slope * tangent_pre


def depthwise(padded, depth_taps, row_count, col_count):
    total = jnp.zeros(padded.shape[:-3] + (row_count, col_count, padded.shape[-1]), jnp.float32)
    for row_off in range(3):
        for col_off in range(3):
            window = padded[..., row_off:row_off + row_count, col_off:col_off + col_count, :].astype(jnp.float32)
            total = total + window * depth_taps[3 * row_off + col_off].astype(jnp.float32)
    return total


def finish(mixed, depth_bias, half):
    primal_mix = mixed[0] + depth_bias.astype(jnp.float32)
    tangent_mix = mixed[1]
    gate_value, gate_tangent = tangent_act(primal_mix[..., half:], tangent_mix[..., half:])
    gated = primal_mix[..., :half] * gate_value
    gated_tangent = tangent_mix[..., :half] * gate_value + primal_mix[..., :half] * gate_tangent
    return gated.astype(jnp.bfloat16), gated_tangent.astype(jnp.bfloat16)


def reference(latents, tangents, w_expand, b_expand, w_depth, b_depth):
    token_count = ROWS * COLS

    def one_image(pair):
        image, image_tangent = pair
        stacked = jnp.concatenate([image.reshape(token_count, C), image_tangent.reshape(token_count, C)], 0)
        pre_act = jnp.dot(stacked, w_expand, preferred_element_type=jnp.float32)
        value, slope_tangent = tangent_act(pre_act[:token_count] + b_expand.astype(jnp.float32), pre_act[token_count:])
        activated = jnp.stack([value.astype(jnp.bfloat16), slope_tangent.astype(jnp.bfloat16)])
        activated = activated.reshape(2, ROWS, COLS, 2 * H)
        padded = jnp.pad(activated, ((0, 0), (1, 1), (1, 1), (0, 0)))
        mixed = depthwise(padded, w_depth, ROWS, COLS)
        return finish(mixed, b_depth, H)

    gated, gated_tangent = lax.map(one_image, (latents, tangents))
    return gated, gated_tangent
```

```python
import jax
import jax.numpy as jnp
from jax import lax
from jax.experimental import pallas as pl
from jax.experimental.pallas import tpu as pltpu
from jax.sharding import PartitionSpec as P


def extended(cells, sides, width):
    for axis, dim in sides:
        count = lax.axis_size(axis)
        ends = count - 1
        head = lax.slice_in_dim(cells, 0, width, axis=dim)
        tail = lax.slice_in_dim(cells, cells.shape[dim] - width, cells.shape[dim], axis=dim)
        cells = jnp.concatenate(
            [
                lax.ppermute(tail, axis, [(i, (i + 1) % count) for i in range(ends)]),
                cells,
                lax.ppermute(head, axis, [((i + 1) % count, i) for i in range(ends)]),
            ],
            axis=dim,
        )
    return cells


def tangent_act(primal_pre, tangent_pre):
    sigmoid_v = jax.nn.sigmoid(primal_pre)
    value = primal_pre * sigmoid_v
    slope = sigmoid_v * (1.0 + primal_pre * (1.0 - sigmoid_v))
    return (value, slope * tangent_pre)


def depthwise(padded, depth_taps, row_count, col_count):
    total = jnp.zeros(padded.shape[:-3] + (row_count, col_count, padded.shape[-1]), jnp.float32)
    for row_off in range(3):
        for col_off in range(3):
            window = padded[
                ..., row_off : row_off + row_count, col_off : col_off + col_count, :
            ].astype(jnp.float32)
            total = total + window * depth_taps[3 * row_off + col_off].astype(jnp.float32)
    return total


def finish(mixed, depth_bias, half):
    primal_mix = mixed[0] + depth_bias.astype(jnp.float32)
    tangent_mix = mixed[1]
    gate_value, gate_tangent = tangent_act(primal_mix[..., half:], tangent_mix[..., half:])
    gated = primal_mix[..., :half] * gate_value
    gated_tangent = tangent_mix[..., :half] * gate_value + primal_mix[..., :half] * gate_tangent
    return (gated.astype(jnp.bfloat16), gated_tangent.astype(jnp.bfloat16))


def activate(pre_act, expand_bias, token_count):
    bias_cols = expand_bias.astype(jnp.float32)
    value, slope_tangent = tangent_act(pre_act[:token_count] + bias_cols, pre_act[token_count:])
    return jnp.concatenate([value.astype(jnp.bfloat16), slope_tangent.astype(jnp.bfloat16)], 0)


def on_device(latents, tangents, w_expand, b_expand, w_depth, b_depth):
    image_count, row_count, col_count, channels = latents.shape
    depth_taps, expand_bias, depth_bias = (
        lax.all_gather(w_depth, "band", axis=1, tiled=True),
        lax.all_gather(b_expand, "band", axis=0, tiled=True),
        lax.all_gather(b_depth, "band", axis=0, tiled=True),
    )
    full_width = expand_bias.shape[0]
    half = full_width // 2
    both_inputs = jnp.stack([latents, tangents])
    both_inputs = extended(both_inputs, (("band", 2),), 1)
    span_rows = both_inputs.shape[2]
    token_count = image_count * span_rows * col_count
    stacked = both_inputs.reshape(2 * token_count, channels)
    weight_rows = lax.all_gather(w_expand, "img", axis=0, tiled=True)
    pre_act = jnp.dot(
        stacked,
        lax.all_gather(weight_rows, "band", axis=1, tiled=True),
        preferred_element_type=jnp.float32,
    )
    activated = activate(pre_act, expand_bias, token_count)
    activated = activated.reshape(2, image_count, span_rows, col_count, full_width)
    band_count = lax.axis_size("band")
    global_row = lax.axis_index("band") * row_count + jnp.arange(span_rows, dtype=jnp.int32) - 1
    inside = (global_row >= 0) & (global_row < band_count * row_count)
    padded = jnp.where(inside[None, None, :, None, None], activated, jnp.zeros_like(activated))
    padded = jnp.pad(padded, ((0, 0), (0, 0), (0, 0), (1, 1), (0, 0)))
    mixed = depthwise(padded, depth_taps, row_count, col_count)
    return finish(mixed, depth_bias, half)


MESH = pl.DeviceIdType.MESH
PIECE = 256


def round_up(size, unit):
    return -(-size // unit) * unit


def act_slope(v):
    sig = jax.nn.sigmoid(v)
    return v * sig, sig * (1.0 + v * (1.0 - sig))


def fused_kernel(
    acts_ref, w_ref, par_ref, out_ref,
    abuf, wbuf, pbuf, ebuf, stage,
    acts_sem, halo_send, halo_recv, par_send, par_recv, w_send, w_recv, out_send, out_recv,
):
    depth = 4
    pieces = w_ref.shape[0]
    rows = acts_ref.shape[1]
    cols = acts_ref.shape[2]
    span = 2 * rows + 2
    img = lax.axis_index("img")
    band = lax.axis_index("band")
    z = band // 2
    core = band % 2
    sib = z * 2 + (1 - core)
    px, py = img % 2, img // 2
    img_x = py * 2 + (1 - px)
    img_y = (1 - py) * 2 + px
    img_d = (1 - py) * 2 + (1 - px)

    barrier = pltpu.get_barrier_semaphore()
    for other in range(1, 2 * depth):
        pl.semaphore_signal(
            barrier, inc=1, device_id=(img, lax.rem(band + other, 2 * depth)), device_id_type=MESH
        )
    for other in (img_x, img_y):
        pl.semaphore_signal(barrier, inc=1, device_id=(other, band), device_id_type=MESH)
    pl.semaphore_wait(barrier, 2 * depth + 1)

    def remote(src, dst, send, recv, device):
        return pltpu.make_async_remote_copy(
            src_ref=src, dst_ref=dst, send_sem=send, recv_sem=recv, device_id=device, device_id_type=MESH
        )

    first = 1 + rows * core
    keep = pltpu.make_async_copy(acts_ref, abuf.at[:, pl.ds(first, rows)], acts_sem.at[0])
    keep.start()
    share = remote(acts_ref, abuf.at[:, pl.ds(first, rows)], acts_sem.at[1], acts_sem.at[2], (img, sib))
    share.start()

    def halo_up(to):
        return remote(
            acts_ref.at[:, rows - 1], abuf.at[:, 0], halo_send.at[to], halo_recv.at[0],
            (img, 2 * (z + 1) + to),
        )

    def halo_down(to):
        return remote(
            acts_ref.at[:, 0], abuf.at[:, span - 1], halo_send.at[to], halo_recv.at[1],
            (img, 2 * (z - 1) + to),
        )

    sends_up = (core == 1) & (z < depth - 1)
    sends_down = (core == 0) & (z > 0)

    @pl.when(sends_up)
    def _():
        halo_up(0).start()
        halo_up(1).start()

    @pl.when(sends_down)
    def _():
        halo_down(0).start()
        halo_down(1).start()

    def par_copy(step):
        to = lax.rem(z + step, depth)
        return remote(par_ref, pbuf.at[z], par_send.at[step], par_recv.at[z], (img, 2 * to + core))

    for step in range(1, depth):
        par_copy(step).start()
    pbuf[z] = par_ref[...]

    def w_copy(route, src, zz, p, column):
        device = (
            (img_x, band), (img_y, band), (img, band + 2), (img, band - 2)
        )[route]
        return remote(
            src, wbuf.at[zz, p, column], w_send.at[route, zz, p, column], w_recv.at[zz, p, column], device
        )

    def arrived(zz, p, column):
        w_copy(0, wbuf.at[zz, p, column], zz, p, column).wait_recv()

    def own_sends(p):
        src = w_ref.at[p]

        @pl.when(z < depth - 1)
        def _():
            w_copy(2, src, z, p, img).start()

        @pl.when(z > 0)
        def _():
            w_copy(3, src, z, p, img).start()

        w_copy(0, src, z, p, img).start()
        w_copy(1, src, z, p, img).start()

    def forward_z(p):
        for dist in range(1, depth):
            @pl.when(z - dist >= 0)
            def _():
                zz = z - dist
                arrived(zz, p, img)

                @pl.when(z < depth - 1)
                def _():
                    w_copy(2, wbuf.at[zz, p, img], zz, p, img).start()

                w_copy(0, wbuf.at[zz, p, img], zz, p, img).start()
                w_copy(1, wbuf.at[zz, p, img], zz, p, img).start()

            @pl.when(z + dist < depth)
            def _():
                zz = z + dist
                arrived(zz, p, img)

                @pl.when(z > 0)
                def _():
                    w_copy(3, wbuf.at[zz, p, img], zz, p, img).start()

                w_copy(0, wbuf.at[zz, p, img], zz, p, img).start()
                w_copy(1, wbuf.at[zz, p, img], zz, p, img).start()

    def forward_xy(p):
        for dist in range(depth):
            zz = lax.rem(z + dist, depth)
            arrived(zz, p, img_x)
            arrived(zz, p, img_y)

            @pl.when(zz % 2 == 0)
            def _():
                w_copy(1, wbuf.at[zz, p, img_x], zz, p, img_x).start()

            @pl.when(zz % 2 == 1)
            def _():
                w_copy(0, wbuf.at[zz, p, img_y], zz, p, img_y).start()

    def out_copy(step):
        p, q = step // 2, step % 2
        return remote(
            stage.at[step], out_ref.at[2 * q + core, p], out_send.at[step], out_recv.at[step], (img, sib)
        )

    row_id = lax.broadcasted_iota(jnp.int32, (cols, 128), 0)

    def compute(step):
        p, q = step // 2, step % 2
        for half in range(2):
            zz = q + (depth // 2) * half
            weights = wbuf[zz, p].reshape(-1, PIECE)

            def product(t, _):
                tokens = abuf[t].reshape(span * cols, -1)
                pre = jnp.dot(tokens, weights, preferred_element_type=jnp.float32)
                ebuf[half, t] = pre.reshape(span, cols, PIECE)
                return 0

            lax.fori_loop(0, 2, product, 0)
            bias = pbuf[zz, p][0:1].astype(jnp.float32)

            def activation(r, _):
                value, slope = act_slope(ebuf[half, 0, r] + bias)
                inside = ((z > 0) | (r > 0)) & ((z < depth - 1) | (r < span - 1))
                scale = jnp.where(inside, 1.0, 0.0)
                ebuf[half, 0, r] = value * scale
                ebuf[half, 1, r] = slope * ebuf[half, 1, r] * scale
                return 0

            lax.fori_loop(0, span, activation, 0)

        par = [pbuf[q, p].astype(jnp.float32), pbuf[q + depth // 2, p].astype(jnp.float32)]

        def mixed(half, t, o, lanes):
            taps = par[half][:, lanes]
            cells = [ebuf[half, t, o + k, :, lanes] for k in range(3)]
            sums = []
            for c in range(3):
                total = cells[0] * taps[1 + c : 2 + c]
                for k in (1, 2):
                    total = total + cells[k] * taps[1 + 3 * k + c : 2 + 3 * k + c]
                sums.append(total)
            before = jnp.where(row_id == 0, 0.0, pltpu.roll(sums[0], 1, 0))
            after = jnp.where(row_id == cols - 1, 0.0, pltpu.roll(sums[2], cols - 1, 0))
            return sums[1] + before + after

        def gate(o, store):
            for lane in range(0, PIECE, 128):
                lanes = slice(lane, lane + 128)
                pv = mixed(0, 0, o, lanes) + par[0][10:11, lanes]
                pg = mixed(1, 0, o, lanes) + par[1][10:11, lanes]
                tv = mixed(0, 1, o, lanes)
                tg = mixed(1, 1, o, lanes)
                value, slope = act_slope(pg)
                store(lanes, (pv * value).astype(jnp.bfloat16), (tv * value + pv * slope * tg).astype(jnp.bfloat16))

        def theirs(j, _):
            def store(lanes, a, b):
                stage[step, 0, j, :, lanes] = a
                stage[step, 1, j, :, lanes] = b

            gate(rows * (1 - core) + j, store)
            return 0

        lax.fori_loop(0, rows, theirs, 0)
        out_copy(step).start()

        def ours(j, _):
            def store(lanes, a, b):
                out_ref[2 * q + core, p, 0, j, :, lanes] = a
                out_ref[2 * q + core, p, 1, j, :, lanes] = b

            gate(rows * core + j, store)
            return 0

        lax.fori_loop(0, rows, ours, 0)

    for p in range(pieces):
        own_sends(p)

    def place(p, _):
        wbuf[z, p, img] = w_ref[p]
        return 0

    lax.fori_loop(0, pieces, place, 0)

    @pl.when(z == 0)
    def _():
        abuf[:, 0] = jnp.zeros(abuf.shape[:1] + abuf.shape[2:], abuf.dtype)

    @pl.when(z == depth - 1)
    def _():
        abuf[:, span - 1] = jnp.zeros(abuf.shape[:1] + abuf.shape[2:], abuf.dtype)

    lax.fori_loop(0, 2, lambda p, _: (forward_z(p), 0)[1], 0)
    forward_xy(0)
    lax.fori_loop(2, pieces, lambda p, _: (forward_z(p), 0)[1], 0)

    keep.wait()
    share.wait()

    @pl.when(z > 0)
    def _():
        halo_up(0).wait_recv()

    @pl.when(z < depth - 1)
    def _():
        halo_down(0).wait_recv()

    for step in range(1, depth):
        source = lax.rem(z + step, depth)
        remote(
            par_ref, pbuf.at[source], par_send.at[step], par_recv.at[source], (img, 2 * source + core)
        ).wait_recv()

    def turn(step, _):
        p, q = step // 2, step % 2

        @pl.when((q == 1) & (p + 1 < pieces))
        def _():
            forward_xy(p + 1)

        arrived(q, p, img_d)
        arrived(q + depth // 2, p, img_d)
        compute(step)
        return 0

    lax.fori_loop(0, 2 * pieces, turn, 0)

    for step in range(1, depth):
        par_copy(step).wait_send()

    @pl.when(sends_up)
    def _():
        halo_up(0).wait_send()
        halo_up(1).wait_send()

    @pl.when(sends_down)
    def _():
        halo_down(0).wait_send()
        halo_down(1).wait_send()

    def sent(p, _):
        for zz in range(depth):
            w_copy(0, w_ref.at[p], zz, p, img).wait_send()
            w_copy(1, w_ref.at[p], zz, p, img).wait_send()
            if zz % 2 == 0:
                w_copy(1, w_ref.at[p], zz, p, img_x).wait_send()
            else:
                w_copy(0, w_ref.at[p], zz, p, img_y).wait_send()

            @pl.when((z >= zz) & (z < depth - 1))
            def _():
                w_copy(2, w_ref.at[p], zz, p, img).wait_send()

            @pl.when((z <= zz) & (z > 0))
            def _():
                w_copy(3, w_ref.at[p], zz, p, img).wait_send()

        return 0

    lax.fori_loop(0, pieces, sent, 0)

    def returned(step, _):
        out_copy(step).wait()
        return 0

    lax.fori_loop(0, 2 * pieces, returned, 0)


def fused(latents, tangents, w_expand, b_expand, w_depth, b_depth):
    _, rows, cols, channels = latents.shape
    part, width = w_expand.shape
    parts = channels // part
    tall = round_up(part, 16)
    pieces = round_up(width, PIECE) // PIECE
    wide = pieces * PIECE
    acts = jnp.stack([latents[0], tangents[0]]).reshape(2, rows, cols, parts, part)
    acts = jnp.pad(acts, ((0, 0),) * 4 + ((0, tall - part),)).reshape(2, rows, cols, parts * tall)
    weights = jnp.pad(w_expand, ((0, tall - part), (0, wide - width)))
    weights = weights.reshape(tall, pieces, PIECE).transpose(1, 0, 2)
    par = jnp.concatenate([b_expand[None], w_depth, b_depth[None]], 0)
    par = jnp.pad(par, ((0, 16 - par.shape[0]), (0, wide - width)))
    par = par.reshape(16, pieces, PIECE).transpose(1, 0, 2)
    bf, f32 = jnp.bfloat16, jnp.float32
    dma = pltpu.SemaphoreType.DMA
    out = pl.pallas_call(
        fused_kernel,
        out_shape=jax.ShapeDtypeStruct((4, pieces, 2, rows, cols, PIECE), bf),
        in_specs=[pl.BlockSpec(memory_space=pltpu.VMEM)] * 3,
        out_specs=pl.BlockSpec(memory_space=pltpu.VMEM),
        scratch_shapes=[
            pltpu.VMEM((2, 2 * rows + 2, cols, parts * tall), bf),
            pltpu.VMEM((4, pieces, parts, tall, PIECE), bf),
            pltpu.VMEM((4, pieces, 16, PIECE), bf),
            pltpu.VMEM((2, 2, 2 * rows + 2, cols, PIECE), f32),
            pltpu.VMEM((2 * pieces, 2, rows, cols, PIECE), bf),
            dma((3,)),
            dma((2,)),
            dma((2,)),
            dma((4,)),
            dma((4,)),
            dma((4, 4, pieces, parts)),
            dma((4, pieces, parts)),
            dma((2 * pieces,)),
            dma((2 * pieces,)),
        ],
        compiler_params=pltpu.CompilerParams(
            collective_id=0, has_side_effects=True, vmem_limit_bytes=40 * 1024 * 1024
        ),
    )(acts, weights, par)
    out = out.transpose(2, 3, 4, 0, 1, 5).reshape(2, rows, cols, 4, wide)[..., :width]
    out = out.reshape(2, 1, rows, cols, 4 * width)
    return out[0], out[1]


def solution(mesh):
    placed = (
        P("img", "band", None, None),
        P("img", "band", None, None),
        P("img", "band"),
        P("band"),
        P(None, "band"),
        P("band"),
    )
    body = on_device
    if mesh.shape["img"] == 4 and mesh.shape["band"] == 8:
        body = fused
    return jax.shard_map(
        body,
        mesh=mesh,
        in_specs=placed,
        out_specs=(P("img", "band", None, None), P("img", "band", None, None)),
        check_vma=False,
    )
```

```python
import jax
import jax.numpy as jnp
from jax import lax
from jax.experimental import pallas as pl
from jax.experimental.pallas import tpu as pltpu
from jax.sharding import PartitionSpec as P


def extended(cells, sides, width):
    for axis, dim in sides:
        count = lax.axis_size(axis)
        ends = count - 1
        head = lax.slice_in_dim(cells, 0, width, axis=dim)
        tail = lax.slice_in_dim(cells, cells.shape[dim] - width, cells.shape[dim], axis=dim)
        cells = jnp.concatenate(
            [
                lax.ppermute(tail, axis, [(i, (i + 1) % count) for i in range(ends)]),
                cells,
                lax.ppermute(head, axis, [((i + 1) % count, i) for i in range(ends)]),
            ],
            axis=dim,
        )
    return cells


def tangent_act(primal_pre, tangent_pre):
    sigmoid_v = jax.nn.sigmoid(primal_pre)
    value = primal_pre * sigmoid_v
    slope = sigmoid_v * (1.0 + primal_pre * (1.0 - sigmoid_v))
    return (value, slope * tangent_pre)


def depthwise(padded, depth_taps, row_count, col_count):
    total = jnp.zeros(padded.shape[:-3] + (row_count, col_count, padded.shape[-1]), jnp.float32)
    for row_off in range(3):
        for col_off in range(3):
            window = padded[
                ..., row_off : row_off + row_count, col_off : col_off + col_count, :
            ].astype(jnp.float32)
            total = total + window * depth_taps[3 * row_off + col_off].astype(jnp.float32)
    return total


def finish(mixed, depth_bias, half):
    primal_mix = mixed[0] + depth_bias.astype(jnp.float32)
    tangent_mix = mixed[1]
    gate_value, gate_tangent = tangent_act(primal_mix[..., half:], tangent_mix[..., half:])
    gated = primal_mix[..., :half] * gate_value
    gated_tangent = tangent_mix[..., :half] * gate_value + primal_mix[..., :half] * gate_tangent
    return (gated.astype(jnp.bfloat16), gated_tangent.astype(jnp.bfloat16))


def activate(pre_act, expand_bias, token_count):
    bias_cols = expand_bias.astype(jnp.float32)
    value, slope_tangent = tangent_act(pre_act[:token_count] + bias_cols, pre_act[token_count:])
    return jnp.concatenate([value.astype(jnp.bfloat16), slope_tangent.astype(jnp.bfloat16)], 0)


def on_device(latents, tangents, w_expand, b_expand, w_depth, b_depth):
    image_count, row_count, col_count, channels = latents.shape
    depth_taps, expand_bias, depth_bias = (
        lax.all_gather(w_depth, "band", axis=1, tiled=True),
        lax.all_gather(b_expand, "band", axis=0, tiled=True),
        lax.all_gather(b_depth, "band", axis=0, tiled=True),
    )
    full_width = expand_bias.shape[0]
    half = full_width // 2
    both_inputs = jnp.stack([latents, tangents])
    both_inputs = extended(both_inputs, (("band", 2),), 1)
    span_rows = both_inputs.shape[2]
    token_count = image_count * span_rows * col_count
    stacked = both_inputs.reshape(2 * token_count, channels)
    weight_rows = lax.all_gather(w_expand, "img", axis=0, tiled=True)
    pre_act = jnp.dot(
        stacked,
        lax.all_gather(weight_rows, "band", axis=1, tiled=True),
        preferred_element_type=jnp.float32,
    )
    activated = activate(pre_act, expand_bias, token_count)
    activated = activated.reshape(2, image_count, span_rows, col_count, full_width)
    band_count = lax.axis_size("band")
    global_row = lax.axis_index("band") * row_count + jnp.arange(span_rows, dtype=jnp.int32) - 1
    inside = (global_row >= 0) & (global_row < band_count * row_count)
    padded = jnp.where(inside[None, None, :, None, None], activated, jnp.zeros_like(activated))
    padded = jnp.pad(padded, ((0, 0), (0, 0), (0, 0), (1, 1), (0, 0)))
    mixed = depthwise(padded, depth_taps, row_count, col_count)
    return finish(mixed, depth_bias, half)


MESH = pl.DeviceIdType.MESH
PIECE = 256


def round_up(size, unit):
    return -(-size // unit) * unit


def act_slope(v):
    sig = jax.nn.sigmoid(v)
    return v * sig, sig * (1.0 + v * (1.0 - sig))


def fused_kernel(
    latents_ref, tangents_ref, w_ref, par_ref, gated_ref, tangent_ref,
    abuf, wbuf, pbuf, ebuf, stage, out_ref, line,
    acts_sem, halo_send, halo_recv, par_send, par_recv, w_send, w_recv, out_send, out_recv,
):
    depth = 4
    pieces = w_ref.shape[1] // PIECE
    _, rows, cols, channels = latents_ref.shape
    parts = wbuf.shape[2]
    span = 2 * rows + 2
    img = lax.axis_index("img")
    band = lax.axis_index("band")
    z = band // 2
    core = band % 2
    sib = z * 2 + (1 - core)
    px, py = img % 2, img // 2
    img_x = py * 2 + (1 - px)
    img_y = (1 - py) * 2 + px
    img_d = (1 - py) * 2 + (1 - px)

    barrier = pltpu.get_barrier_semaphore()
    for other in range(1, 2 * depth):
        pl.semaphore_signal(
            barrier, inc=1, device_id=(img, lax.rem(band + other, 2 * depth)), device_id_type=MESH
        )
    for other in (img_x, img_y):
        pl.semaphore_signal(barrier, inc=1, device_id=(other, band), device_id_type=MESH)
    pl.semaphore_wait(barrier, 2 * depth + 1)

    def remote(src, dst, send, recv, device):
        return pltpu.make_async_remote_copy(
            src_ref=src, dst_ref=dst, send_sem=send, recv_sem=recv, device_id=device, device_id_type=MESH
        )

    def w_copy(route, src, zz, p, column):
        device = (
            (img_x, band), (img_y, band), (img, band + 2), (img, band - 2)
        )[route]
        return remote(
            src, wbuf.at[zz, p, column], w_send.at[route, zz, p, column], w_recv.at[zz, p, column], device
        )

    def arrived(zz, p, column):
        w_copy(0, wbuf.at[zz, p, column], zz, p, column).wait_recv()

    def piece_of(p):
        return w_ref.at[:, pl.ds(pl.multiple_of(p * PIECE, PIECE), PIECE)]

    def own_sends(p):
        src = piece_of(p)

        @pl.when(z < depth - 1)
        def _():
            w_copy(2, src, z, p, img).start()

        @pl.when(z > 0)
        def _():
            w_copy(3, src, z, p, img).start()

        w_copy(0, src, z, p, img).start()
        w_copy(1, src, z, p, img).start()

    for p in range(pieces):
        own_sends(p)

    first = 1 + rows * core
    part = channels // parts
    tall = w_ref.shape[0]
    lane_id = lax.broadcasted_iota(jnp.int32, line.shape, 1)
    line[:, channels:] = jnp.zeros((cols, line.shape[1] - channels), jnp.float32)
    for t, source_ref in enumerate((latents_ref, tangents_ref)):
        for r in range(rows):
            line[:, :channels] = source_ref[0, r].astype(jnp.float32)
            cells = line[...]
            spread = cells
            for i in range(1, parts):
                spread = jnp.where(lane_id >= tall * i, pltpu.roll(cells, (tall - part) * i, 1), spread)
            abuf[t, first + r] = spread.astype(jnp.bfloat16)
    own_rows = abuf.at[:, pl.ds(first, rows)]
    share = remote(own_rows, own_rows, acts_sem.at[0], acts_sem.at[1], (img, sib))
    share.start()

    def halo_up(to):
        return remote(
            abuf.at[:, first + rows - 1], abuf.at[:, 0], halo_send.at[to], halo_recv.at[0],
            (img, 2 * (z + 1) + to),
        )

    def halo_down(to):
        return remote(
            abuf.at[:, first], abuf.at[:, span - 1], halo_send.at[to], halo_recv.at[1],
            (img, 2 * (z - 1) + to),
        )

    sends_up = (core == 1) & (z < depth - 1)
    sends_down = (core == 0) & (z > 0)

    @pl.when(sends_up)
    def _():
        halo_up(0).start()
        halo_up(1).start()

    @pl.when(sends_down)
    def _():
        halo_down(0).start()
        halo_down(1).start()

    def par_copy(step):
        to = lax.rem(z + step, depth)
        return remote(par_ref, pbuf.at[z], par_send.at[step], par_recv.at[z], (img, 2 * to + core))

    for step in range(1, depth):
        par_copy(step).start()
    pbuf[z] = par_ref[...]

    def forward_z(p):
        for dist in range(1, depth):
            @pl.when(z - dist >= 0)
            def _():
                zz = z - dist
                arrived(zz, p, img)

                @pl.when(z < depth - 1)
                def _():
                    w_copy(2, wbuf.at[zz, p, img], zz, p, img).start()

                w_copy(0, wbuf.at[zz, p, img], zz, p, img).start()
                w_copy(1, wbuf.at[zz, p, img], zz, p, img).start()

            @pl.when(z + dist < depth)
            def _():
                zz = z + dist
                arrived(zz, p, img)

                @pl.when(z > 0)
                def _():
                    w_copy(3, wbuf.at[zz, p, img], zz, p, img).start()

                w_copy(0, wbuf.at[zz, p, img], zz, p, img).start()
                w_copy(1, wbuf.at[zz, p, img], zz, p, img).start()

    def forward_xy(p):
        for dist in range(depth):
            zz = lax.rem(z + dist, depth)
            arrived(zz, p, img_x)
            arrived(zz, p, img_y)

            @pl.when((zz % 2 == z % 2) & (zz < depth // 2))
            def _():
                w_copy(1, wbuf.at[zz, p, img_x], zz, p, img_x).start()

            @pl.when((zz % 2 == z % 2) & (zz >= depth // 2))
            def _():
                w_copy(0, wbuf.at[zz, p, img_y], zz, p, img_y).start()

    def forward_diagonal(p):
        for zz in range(depth):
            @pl.when(zz % 2 == z % 2)
            def _():
                arrived(zz, p, img_d)

                @pl.when(z % 2 == 0)
                def _():
                    w_copy(2, wbuf.at[zz, p, img_d], zz, p, img_d).start()

                @pl.when(z % 2 == 1)
                def _():
                    w_copy(3, wbuf.at[zz, p, img_d], zz, p, img_d).start()

    def take_diagonal(zz, p):
        @pl.when(zz % 2 != z % 2)
        def _():
            arrived(zz, p, img_d)

    def out_copy(step):
        p, q = step // 2, step % 2
        return remote(
            stage.at[step], out_ref.at[2 * q + core, p], out_send.at[step], out_recv.at[step], (img, sib)
        )

    row_id = lax.broadcasted_iota(jnp.int32, (cols, 128), 0)

    def params(zz, p):
        return pbuf[zz, :, pl.ds(pl.multiple_of(p * PIECE, PIECE), PIECE)].astype(jnp.float32)

    def compute(step):
        p, q = step // 2, step % 2
        for half in range(2):
            zz = q + (depth // 2) * half
            weights = wbuf[zz, p].reshape(-1, PIECE)

            def product(t, _):
                tokens = abuf[t].reshape(span * cols, -1)
                pre = jnp.dot(tokens, weights, preferred_element_type=jnp.float32)
                ebuf[half, t] = pre.reshape(span, cols, PIECE)
                return 0

            lax.fori_loop(0, 2, product, 0)
            bias = params(zz, p)[0:1]

            def activation(r, _):
                value, slope = act_slope(ebuf[half, 0, r] + bias)
                inside = ((z > 0) | (r > 0)) & ((z < depth - 1) | (r < span - 1))
                scale = jnp.where(inside, 1.0, 0.0)
                ebuf[half, 0, r] = value * scale
                ebuf[half, 1, r] = slope * ebuf[half, 1, r] * scale
                return 0

            lax.fori_loop(0, span, activation, 0)

        par = [params(q, p), params(q + depth // 2, p)]

        def mixed(half, t, o, lanes):
            taps = par[half][:, lanes]
            cells = [ebuf[half, t, o + k, :, lanes] for k in range(3)]
            sums = []
            for c in range(3):
                total = cells[0] * taps[1 + c : 2 + c]
                for k in (1, 2):
                    total = total + cells[k] * taps[1 + 3 * k + c : 2 + 3 * k + c]
                sums.append(total)
            before = jnp.where(row_id == 0, 0.0, pltpu.roll(sums[0], 1, 0))
            after = jnp.where(row_id == cols - 1, 0.0, pltpu.roll(sums[2], cols - 1, 0))
            return sums[1] + before + after

        def gate(o, store):
            for lane in range(0, PIECE, 128):
                lanes = slice(lane, lane + 128)
                pv = mixed(0, 0, o, lanes) + par[0][10:11, lanes]
                pg = mixed(1, 0, o, lanes) + par[1][10:11, lanes]
                tv = mixed(0, 1, o, lanes)
                tg = mixed(1, 1, o, lanes)
                value, slope = act_slope(pg)
                store(lanes, (pv * value).astype(jnp.bfloat16), (tv * value + pv * slope * tg).astype(jnp.bfloat16))

        def theirs(j, _):
            def store(lanes, a, b):
                stage[step, 0, j, :, lanes] = a
                stage[step, 1, j, :, lanes] = b

            gate(rows * (1 - core) + j, store)
            return 0

        lax.fori_loop(0, rows, theirs, 0)
        out_copy(step).start()

        def ours(j, _):
            def store(lanes, a, b):
                out_ref[2 * q + core, p, 0, j, :, lanes] = a
                out_ref[2 * q + core, p, 1, j, :, lanes] = b

            gate(rows * core + j, store)
            return 0

        lax.fori_loop(0, rows, ours, 0)

    for p in range(pieces):
        wbuf[z, p, img] = w_ref[:, p * PIECE : (p + 1) * PIECE]

    @pl.when(z == 0)
    def _():
        abuf[:, 0] = jnp.zeros(abuf.shape[:1] + abuf.shape[2:], abuf.dtype)

    @pl.when(z == depth - 1)
    def _():
        abuf[:, span - 1] = jnp.zeros(abuf.shape[:1] + abuf.shape[2:], abuf.dtype)

    lax.fori_loop(0, 2, lambda p, _: (forward_z(p), 0)[1], 0)
    forward_xy(0)
    lax.fori_loop(2, pieces, lambda p, _: (forward_z(p), 0)[1], 0)

    share.wait()

    @pl.when(z > 0)
    def _():
        halo_up(0).wait_recv()

    @pl.when(z < depth - 1)
    def _():
        halo_down(0).wait_recv()

    for step in range(1, depth):
        source = lax.rem(z + step, depth)
        remote(
            par_ref, pbuf.at[source], par_send.at[step], par_recv.at[source], (img, 2 * source + core)
        ).wait_recv()

    def turn(step, _):
        p, q = step // 2, step % 2

        @pl.when((q == 1) & (p + 1 < pieces))
        def _():
            forward_xy(p + 1)

        @pl.when(q == 0)
        def _():
            forward_diagonal(p)

        take_diagonal(q, p)
        take_diagonal(q + depth // 2, p)
        compute(step)
        return 0

    lax.fori_loop(0, 2 * pieces, turn, 0)

    for step in range(1, depth):
        par_copy(step).wait_send()

    @pl.when(sends_up)
    def _():
        halo_up(0).wait_send()
        halo_up(1).wait_send()

    @pl.when(sends_down)
    def _():
        halo_down(0).wait_send()
        halo_down(1).wait_send()

    def sent(p, _):
        for zz in range(depth):
            w_copy(0, piece_of(p), zz, p, img).wait_send()
            w_copy(1, piece_of(p), zz, p, img).wait_send()

            @pl.when(zz % 2 == z % 2)
            def _():
                if zz < depth // 2:
                    w_copy(1, piece_of(p), zz, p, img_x).wait_send()
                else:
                    w_copy(0, piece_of(p), zz, p, img_y).wait_send()

                @pl.when(z % 2 == 0)
                def _():
                    w_copy(2, piece_of(p), zz, p, img_d).wait_send()

                @pl.when(z % 2 == 1)
                def _():
                    w_copy(3, piece_of(p), zz, p, img_d).wait_send()

            @pl.when((z >= zz) & (z < depth - 1))
            def _():
                w_copy(2, piece_of(p), zz, p, img).wait_send()

            @pl.when((z <= zz) & (z > 0))
            def _():
                w_copy(3, piece_of(p), zz, p, img).wait_send()

        return 0

    lax.fori_loop(0, pieces, sent, 0)

    def returned(step, _):
        out_copy(step).wait()
        return 0

    lax.fori_loop(0, 2 * pieces, returned, 0)

    tiles = gated_ref.shape[3] // 128 // 2
    met = tiles // 2

    def finished(j, _):
        for which, ref in enumerate((gated_ref, tangent_ref)):
            for q in range(depth // 2):
                for tile in range(tiles):
                    blocks = []
                    for side, index in ((0, tile), (1, tile - met)):
                        if 0 <= index <= met:
                            lanes = slice(index * 128 % PIECE, index * 128 % PIECE + 128)
                            blocks.append(out_ref[2 * q + side, index * 128 // PIECE, which, j, :, lanes])
                    block = blocks[0] if len(blocks) == 1 else blocks[0] + blocks[1]
                    lane = (q * tiles + tile) * 128
                    ref[0, j, :, lane : lane + 128] = block
        return 0

    lax.fori_loop(0, rows, finished, 0)


def fused(latents, tangents, w_expand, b_expand, w_depth, b_depth):
    _, rows, cols, channels = latents.shape
    part, width = w_expand.shape
    parts = channels // part
    tall = round_up(part, 16)
    pieces = round_up(width, PIECE) // PIECE
    wide = pieces * PIECE
    gap = (wide - width) * (lax.axis_index("band") % 2)
    weights = lax.dynamic_update_slice(jnp.zeros((tall, wide), w_expand.dtype), w_expand, (0, gap))
    par = jnp.concatenate([b_expand[None], w_depth, b_depth[None]], 0)
    par = lax.dynamic_update_slice(jnp.zeros((16, wide), par.dtype), par, (0, gap))
    bf, f32 = jnp.bfloat16, jnp.float32
    dma = pltpu.SemaphoreType.DMA
    result = jax.ShapeDtypeStruct((1, rows, cols, 4 * width), bf)
    return pl.pallas_call(
        fused_kernel,
        out_shape=(result, result),
        in_specs=[pl.BlockSpec(memory_space=pltpu.VMEM)] * 4,
        out_specs=[pl.BlockSpec(memory_space=pltpu.VMEM)] * 2,
        scratch_shapes=[
            pltpu.VMEM((2, 2 * rows + 2, cols, parts * tall), bf),
            pltpu.VMEM((4, pieces, parts, tall, PIECE), bf),
            pltpu.VMEM((4, 16, wide), bf),
            pltpu.VMEM((2, 2, 2 * rows + 2, cols, PIECE), f32),
            pltpu.VMEM((2 * pieces, 2, rows, cols, PIECE), bf),
            pltpu.VMEM((4, pieces, 2, rows, cols, PIECE), bf),
            pltpu.VMEM((cols, parts * tall), f32),
            dma((2,)),
            dma((2,)),
            dma((2,)),
            dma((4,)),
            dma((4,)),
            dma((4, 4, pieces, parts)),
            dma((4, pieces, parts)),
            dma((2 * pieces,)),
            dma((2 * pieces,)),
        ],
        compiler_params=pltpu.CompilerParams(
            collective_id=0, has_side_effects=True, vmem_limit_bytes=40 * 1024 * 1024
        ),
    )(latents, tangents, weights, par)


def solution(mesh):
    placed = (
        P("img", "band", None, None),
        P("img", "band", None, None),
        P("img", "band"),
        P("band"),
        P(None, "band"),
        P("band"),
    )
    body = on_device
    if mesh.shape["img"] == 4 and mesh.shape["band"] == 8:
        body = fused
    return jax.shard_map(
        body,
        mesh=mesh,
        in_specs=placed,
        out_specs=(P("img", "band", None, None), P("img", "band", None, None)),
        check_vma=False,
    )
```
